256 devices in a mesh: grp: 8 (over y, core), fsdp: 32 (over z, x).
Axes of the slice: x: 4, y: 4, z: 8, core: 2. Of those that a mesh axis runs over, the one named last changes fastest.
Arguments:
- gradient: float32 [8, 2048, 7168], P('grp', None, 'fsdp'), may hold values from -20000 to 20000
- master: float32 [8, 2048, 7168], P('grp', 'fsdp'), may hold values from -6 to 6
- first_moment: float32 [8, 2048, 7168], P('grp', 'fsdp'), may hold values from -0.3 to 0.3
- second_moment: float32 [8, 2048, 7168], P('grp', 'fsdp'), may hold values from 0.0005 to 0.05
- slot_expert: int32 [8, 4], P('grp'), may hold values from -1 to 7, as said below
Outputs:
- rollout: bfloat16 [32, 2048, 7168], P('grp', None, 'fsdp')
The draws below stay inside these ranges and needn't reach their ends.
Inputs may be any that keep to these rules, and one draw needn't show every extreme that they name: `slot_expert`: each rollout group has 4 slots; its live slots come first and the rest hold -1; no expert stands twice in one group; every expert stands in at least one slot; at least one group has all 4 slots live.
All inputs are finite; a program needn't handle non-finite values.
Results may differ from the reference program's by a relative error of at most 0.00185.
Values may be sent and summed in bfloat16 or wider, within the bound.
No kernel may reach another device: no remote copies, remote signals or barrier semaphores. Data moves between devices by JAX's collectives and lax.ppermute only.
A program may use at most 128 MiB of HBM per device.

```python
import math
import jax
import jax.numpy as jnp
from jax import lax

D = 7168
FF = 2048
SLOTS = 4
EXPERTS = 8
N_GRP = 8


def draw_gradient(key, part):
    key = jax.random.fold_in(key, 5)
    value_key, row_key, column_key = jax.random.split(key, 3)
    expert_pos = jnp.arange(EXPERTS, dtype=jnp.float32) / max(EXPERTS - 1, 1)
    column_pos = jnp.arange(D, dtype=jnp.float32) / (D - 1)
    scale_top = 10.0
    values = jax.random.normal(value_key, (EXPERTS, FF, D), jnp.float32)
    row_scale = scale_top ** jax.random.uniform(row_key, (EXPERTS, FF, 1), jnp.float32)
    column_scale = scale_top ** jax.random.uniform(column_key, (EXPERTS, 1, D), jnp.float32)
    ramp_scale = (1.0 + expert_pos)[:, None, None] * (1.0 + column_pos)[None, None, :]
    return values * row_scale * column_scale * ramp_scale


def draw_slot_expert(key, part):
    key = jax.random.fold_in(key, 11)
    anchor_key, hot_key, level_key, jitter_key, count_key, full_key = jax.random.split(key, 6)
    anchor = jax.random.permutation(anchor_key, EXPERTS)
    hot_order = jax.random.permutation(hot_key, EXPERTS)
    hotness = jnp.where(hot_order < 2, 8, 0) + jax.random.randint(level_key, (EXPERTS,), 0, 3)
    jitter = jax.random.randint(jitter_key, (N_GRP, EXPERTS), 0, 1024)
    expert_index = jnp.arange(EXPERTS, dtype=jnp.int32)
    ranking = (hotness[None, :] * 1024 + jitter) * EXPERTS + expert_index[None, :]
    ranking = ranking + jnp.where(expert_index[None, :] == anchor[:, None], 1 << 24, 0)
    _, chosen = jax.lax.top_k(ranking, SLOTS)
    counts = jax.random.randint(count_key, (N_GRP,), 1, SLOTS + 1)
    full_group = jax.random.randint(full_key, (), 0, N_GRP)
    counts = jnp.where(jnp.arange(N_GRP) == full_group, SLOTS, counts)
    live = jnp.arange(SLOTS)[None, :] < counts[:, None]
    return jnp.where(live, chosen, -1).astype(jnp.int32)


def block_scale(own_key, dims, cuts, low, largest):
    loudness, own = 1.0, jax.random.fold_in(own_key, 6)
    for axis_at, parts in cuts:
        draws = jnp.exp(jax.random.uniform(jax.random.fold_in(own, axis_at), (parts,), jnp.float32, low / len(cuts), largest / len(cuts)))
        loudness = loudness * jnp.repeat(draws, dims[axis_at] // parts).reshape([-1 if axis == axis_at else 1 for axis in range(len(dims))])
    return loudness


def scatter_about(rng, dims, scale, most, cuts=(), kind=jnp.bfloat16):
    array = scale * jax.random.normal(rng, dims, jnp.float32)
    if cuts:
        array = array * block_scale(rng, dims, cuts, -0.22, 0.18)
    return jnp.clip(array, -most, most).astype(kind)


def setup_inputs(seed: int = 0) -> dict:
    key_list = jax.random.split(jax.random.key(seed), 6)
    return {
        "gradient": draw_gradient(jax.random.fold_in(key_list[5], 71), 0),
        "master": scatter_about(key_list[1], (EXPERTS, FF, D), 1.0, 6.0, ((0, 8), (1, 32)), jnp.float32),
        "first_moment": scatter_about(key_list[2], (EXPERTS, FF, D), 0.05, 0.3, ((0, 8), (1, 32)), jnp.float32),
        "second_moment": jnp.clip(jnp.exp(math.log(0.05) - 4.6051702 * jax.random.uniform(key_list[3], (EXPERTS, FF, D), jnp.float32) ** block_scale(key_list[3], (EXPERTS, FF, D), ((0, 8), (1, 32)), -0.2, 0.2)), 0.0005, 0.05),
        "slot_expert": draw_slot_expert(jax.random.fold_in(key_list[5], 71), 0),
    }


first_decay = 0.9
second_decay = 0.95
first_bias = 1.0 - 0.9 ** 10
second_bias = 1.0 - 0.95 ** 10
learn_rate = 0.2
shrink = 0.98
epsilon = 1e-08
stabilizer = 1e-06
clip_level = 1.0

def adam_weights(gradient, master, first_moment, second_moment, factor):
    scaled = factor * gradient
    first_new = first_decay * first_moment + (1.0 - first_decay) * scaled
    second_new = second_decay * second_moment + (1.0 - second_decay) * scaled * scaled
    update = first_new / first_bias / (jnp.sqrt(second_new / second_bias) + epsilon)
    return (shrink * master - learn_rate * update).astype(jnp.bfloat16)

def reference(gradient, master, first_moment, second_moment, slot_expert):
    entries = EXPERTS * FF * D
    squares = lax.map(lambda matrix: jnp.sum(matrix * matrix), gradient)
    square_total = jnp.sum(squares)
    factor = jnp.minimum(1.0, clip_level / jnp.sqrt(square_total / entries + stabilizer))

    def one_expert(operands):
        return adam_weights(operands[0], operands[1], operands[2], operands[3], factor)
    weights = lax.map(one_expert, (gradient, master, first_moment, second_moment))
    flat_ids = slot_expert.reshape(-1).astype(jnp.int32)
    clipped_ids = jnp.clip(flat_ids, 0, EXPERTS - 1).astype(jnp.int32)
    picked = jnp.take(weights, clipped_ids, axis=0)
    return jnp.where((flat_ids >= 0)[:, None, None], picked, jnp.zeros((), jnp.bfloat16))
```

```python
import functools

import jax
import jax.numpy as jnp
from jax import lax
from jax.experimental import pallas as pl
from jax.experimental.pallas import tpu as pltpu
from jax.sharding import PartitionSpec as P

D = 7168
FF = 2048


first_decay = 0.9
second_decay = 0.95
first_bias = 1.0 - 0.9**10
second_bias = 1.0 - 0.95**10
learn_rate = 0.2
shrink = 0.98
epsilon = 1e-08
stabilizer = 1e-06
clip_level = 1.0

LANES = 128
HALF = 64
VMEM_LIMIT = 48 * 1024 * 1024


def low_halves(a, b):
    return jnp.concatenate([a[:, :HALF], b[:, :HALF]], axis=1)


def high_halves(a, b):
    return jnp.concatenate([a[:, HALF:], b[:, HALF:]], axis=1)


def pack_kernel(grad_ref, block_ref, square_ref):
    step = pl.program_id(0)
    middle = grad_ref.shape[0] // 2
    squares = jnp.zeros((8, LANES), jnp.float32)
    for pair in range(grad_ref.shape[1] // LANES):
        lanes = slice(LANES * pair, LANES * (pair + 1))
        first, second = grad_ref[:middle, lanes], grad_ref[middle:, lanes]
        squares += jnp.sum((first * first + second * second).reshape(-1, 8, LANES), axis=0)
        block_ref[2 * pair] = low_halves(first, second).astype(jnp.bfloat16)
        block_ref[2 * pair + 1] = high_halves(first, second).astype(jnp.bfloat16)

    squares = jnp.sum(squares, axis=0, keepdims=True)

    @pl.when(step == 0)
    def _():
        square_ref[...] = squares

    @pl.when(step > 0)
    def _():
        square_ref[...] += squares


def pack(grad_columns):
    columns, rows = grad_columns.shape
    steps = 4
    return pl.pallas_call(
        pack_kernel,
        grid=(steps,),
        in_specs=[pl.BlockSpec((columns, rows // steps), lambda i: (0, i))],
        out_specs=[
            pl.BlockSpec((rows // HALF // steps, columns // 2, LANES), lambda i: (i, 0, 0)),
            pl.BlockSpec((1, LANES), lambda i: (0, 0)),
        ],
        out_shape=[
            jax.ShapeDtypeStruct((rows // HALF, columns // 2, LANES), jnp.bfloat16),
            jax.ShapeDtypeStruct((1, LANES), jnp.float32),
        ],
        compiler_params=pltpu.CompilerParams(vmem_limit_bytes=VMEM_LIMIT),
    )(grad_columns)


def adam_weights(gradient, master, first_moment, second_moment, factor):
    scaled = factor * gradient
    first_new = first_decay * first_moment + (1.0 - first_decay) * scaled
    second_new = second_decay * second_moment + (1.0 - second_decay) * scaled * scaled
    update = first_new / first_bias / (jnp.sqrt(second_new / second_bias) + epsilon)
    return shrink * master - learn_rate * update


def adam_kernel(entries, squares_ref, grad_ref, master_ref, first_ref, second_ref, out_ref, flat_ref):
    sources, middle = grad_ref.shape[0], grad_ref.shape[1]
    square_total = jnp.sum(squares_ref[...])
    factor = jnp.minimum(1.0, clip_level / jnp.sqrt(square_total / entries + stabilizer))
    half_sources = sources // 2
    for s in range(half_sources):
        low, high = grad_ref[s].astype(jnp.float32), grad_ref[half_sources + s].astype(jnp.float32)
        at = 2 * middle * s
        flat_ref[at : at + middle] = low_halves(low, high)
        flat_ref[at + middle : at + 2 * middle] = high_halves(low, high)
    count = flat_ref.shape[0]
    for j in range(count // LANES):
        here = slice(LANES * j, LANES * (j + 1))
        there = slice(count + LANES * j, count + LANES * (j + 1))
        both = lambda ref: jnp.concatenate([ref[:, here], ref[:, there]], axis=0)
        weights = adam_weights(flat_ref[here].T, both(master_ref), both(first_ref), both(second_ref), factor)
        flat_ref[here] = weights.T
    for s in range(half_sources):
        at = 2 * middle * s
        first, second = flat_ref[at : at + middle], flat_ref[at + middle : at + 2 * middle]
        out_ref[s] = low_halves(first, second).astype(jnp.bfloat16)
        out_ref[half_sources + s] = high_halves(first, second).astype(jnp.bfloat16)


def adam(entries, squares, grad_blocks, master, first_moment, second_moment):
    peers, middle, _ = grad_blocks.shape
    steps = 4
    state = pl.BlockSpec((HALF, D // steps), lambda i: (0, i))
    blocks = pl.BlockSpec((peers // steps, middle, LANES), lambda i: (i, 0, 0))
    return pl.pallas_call(
        functools.partial(adam_kernel, entries),
        grid=(steps,),
        in_specs=[pl.BlockSpec((1, LANES), lambda i: (0, 0)), blocks, state, state, state],
        out_specs=blocks,
        out_shape=jax.ShapeDtypeStruct(grad_blocks.shape, jnp.bfloat16),
        scratch_shapes=[pltpu.VMEM((D // steps // 2, LANES), jnp.float32)],
        compiler_params=pltpu.CompilerParams(vmem_limit_bytes=VMEM_LIMIT),
    )(squares, grad_blocks, master, first_moment, second_moment)


def place_kernel(slot_ref, block_ref, out_ref):
    live = slot_ref[pl.program_id(0)] >= 0
    middle = block_ref.shape[2]

    @pl.when(live)
    def _():
        for pair in range(block_ref.shape[1] // 2):
            lanes = slice(LANES * pair, LANES * (pair + 1))
            first = block_ref[0, 2 * pair].astype(jnp.float32)
            second = block_ref[0, 2 * pair + 1].astype(jnp.float32)
            out_ref[0, :middle, lanes] = low_halves(first, second).astype(jnp.bfloat16)
            out_ref[0, middle:, lanes] = high_halves(first, second).astype(jnp.bfloat16)

    @pl.when(jnp.logical_not(live))
    def _():
        out_ref[...] = jnp.zeros_like(out_ref)


def place(slot_ids, experts):
    n_experts, peers, middle, _ = experts.shape
    slots = slot_ids.shape[0]
    steps = 2
    return pl.pallas_call(
        place_kernel,
        grid_spec=pltpu.PrefetchScalarGridSpec(
            num_scalar_prefetch=1,
            grid=(slots, steps),
            in_specs=[
                pl.BlockSpec(
                    (1, peers // steps, middle, LANES),
                    lambda s, i, ids: (jnp.clip(ids[s], 0, n_experts - 1), i, 0, 0),
                )
            ],
            out_specs=pl.BlockSpec((1, 2 * middle, peers * HALF // steps), lambda s, i, ids: (s, 0, i)),
        ),
        out_shape=jax.ShapeDtypeStruct((slots, 2 * middle, peers * HALF), jnp.bfloat16),
        compiler_params=pltpu.CompilerParams(vmem_limit_bytes=VMEM_LIMIT),
    )(slot_ids, experts)


def total_everywhere(partial):
    for axis in ("grp", "fsdp"):
        size, apart = lax.axis_size(axis), 1
        while apart < size:
            partial += lax.ppermute(partial, axis, [(i, i ^ apart) for i in range(size)])
            apart *= 2
    return partial


def body(gradient, master, first_moment, second_moment, slot_expert):
    entries = lax.axis_size("grp") * master.shape[0] * FF * D
    slot_ids = slot_expert.reshape(-1)
    grad_blocks, squares = pack(jnp.swapaxes(gradient[0], 0, 1))
    grad_here = lax.all_to_all(grad_blocks, "fsdp", 0, 0, tiled=True)
    squares = total_everywhere(squares)
    weights = adam(entries, squares, grad_here, master[0], first_moment[0], second_moment[0])
    columns = lax.all_to_all(weights, "fsdp", 0, 0, tiled=True)
    experts = lax.all_gather(columns, "grp", axis=0, tiled=False)
    rollout = place(slot_ids, experts)
    return jnp.swapaxes(rollout, 1, 2)


def solution(mesh):
    in_specs = (
        P("grp", None, "fsdp"),
        P("grp", "fsdp", None),
        P("grp", "fsdp", None),
        P("grp", "fsdp", None),
        P("grp", None),
    )
    out_specs = P("grp", None, "fsdp")
    return jax.shard_map(body, mesh=mesh, in_specs=in_specs, out_specs=out_specs, check_vma=False)
```

```python
import functools

import jax
import jax.numpy as jnp
from jax import lax
from jax.experimental import pallas as pl
from jax.experimental.pallas import tpu as pltpu
from jax.sharding import PartitionSpec as P

D = 7168
FF = 2048


first_decay = 0.9
second_decay = 0.95
first_bias = 1.0 - 0.9**10
second_bias = 1.0 - 0.95**10
learn_rate = 0.2
shrink = 0.98
epsilon = 1e-08
stabilizer = 1e-06
clip_level = 1.0

LANES = 128
HALF = 64
VMEM_LIMIT = 16 * 1024 * 1024


def low_halves(a, b):
    return jnp.concatenate([a[:, :HALF], b[:, :HALF]], axis=1)


def high_halves(a, b):
    return jnp.concatenate([a[:, HALF:], b[:, HALF:]], axis=1)


def pack_kernel(grad_ref, block_ref, square_ref):
    step = pl.program_id(0)
    middle = grad_ref.shape[0] // 2
    squares = jnp.zeros((8, LANES), jnp.float32)
    for pair in range(grad_ref.shape[1] // LANES):
        lanes = slice(LANES * pair, LANES * (pair + 1))
        first, second = grad_ref[:middle, lanes], grad_ref[middle:, lanes]
        squares += jnp.sum((first * first + second * second).reshape(-1, 8, LANES), axis=0)
        block_ref[2 * pair] = low_halves(first, second).astype(jnp.bfloat16)
        block_ref[2 * pair + 1] = high_halves(first, second).astype(jnp.bfloat16)

    squares = jnp.sum(squares, axis=0, keepdims=True)

    @pl.when(step == 0)
    def _():
        square_ref[...] = squares

    @pl.when(step > 0)
    def _():
        square_ref[...] += squares


def pack(grad_columns):
    columns, rows = grad_columns.shape
    steps = 4
    return pl.pallas_call(
        pack_kernel,
        grid=(steps,),
        in_specs=[pl.BlockSpec((columns, rows // steps), lambda i: (0, i))],
        out_specs=[
            pl.BlockSpec((rows // HALF // steps, columns // 2, LANES), lambda i: (i, 0, 0)),
            pl.BlockSpec((1, LANES), lambda i: (0, 0)),
        ],
        out_shape=[
            jax.ShapeDtypeStruct((rows // HALF, columns // 2, LANES), jnp.bfloat16),
            jax.ShapeDtypeStruct((1, LANES), jnp.float32),
        ],
        compiler_params=pltpu.CompilerParams(vmem_limit_bytes=VMEM_LIMIT),
    )(grad_columns)


def adam_weights(gradient, master, first_moment, second_moment, factor):
    scaled = factor * gradient
    first_new = first_decay * first_moment + (1.0 - first_decay) * scaled
    second_new = second_decay * second_moment + (1.0 - second_decay) * scaled * scaled
    update = first_new / first_bias / (jnp.sqrt(second_new / second_bias) + epsilon)
    return shrink * master - learn_rate * update


def adam_kernel(entries, squares_ref, grad_ref, master_ref, first_ref, second_ref, out_ref, flat_ref):
    sources, middle = grad_ref.shape[0], grad_ref.shape[1]
    square_total = jnp.sum(squares_ref[...])
    factor = jnp.minimum(1.0, clip_level / jnp.sqrt(square_total / entries + stabilizer))
    half_sources = sources // 2
    for s in range(half_sources):
        low, high = grad_ref[s].astype(jnp.float32), grad_ref[half_sources + s].astype(jnp.float32)
        at = 2 * middle * s
        flat_ref[at : at + middle] = low_halves(low, high)
        flat_ref[at + middle : at + 2 * middle] = high_halves(low, high)
    count = flat_ref.shape[0]
    for j in range(count // LANES):
        here = slice(LANES * j, LANES * (j + 1))
        there = slice(count + LANES * j, count + LANES * (j + 1))
        both = lambda ref: jnp.concatenate([ref[:, here], ref[:, there]], axis=0)
        weights = adam_weights(flat_ref[here].T, both(master_ref), both(first_ref), both(second_ref), factor)
        flat_ref[here] = weights.T
    for s in range(half_sources):
        at = 2 * middle * s
        first, second = flat_ref[at : at + middle], flat_ref[at + middle : at + 2 * middle]
        out_ref[s] = low_halves(first, second).astype(jnp.bfloat16)
        out_ref[half_sources + s] = high_halves(first, second).astype(jnp.bfloat16)


def adam(entries, squares, grad_blocks, master, first_moment, second_moment):
    peers, middle, _ = grad_blocks.shape
    steps = 4
    state = pl.BlockSpec((HALF, D // steps), lambda i: (0, i))
    blocks = pl.BlockSpec((peers // steps, middle, LANES), lambda i: (i, 0, 0))
    return pl.pallas_call(
        functools.partial(adam_kernel, entries),
        grid=(steps,),
        in_specs=[pl.BlockSpec((1, LANES), lambda i: (0, 0)), blocks, state, state, state],
        out_specs=blocks,
        out_shape=jax.ShapeDtypeStruct(grad_blocks.shape, jnp.bfloat16),
        scratch_shapes=[pltpu.VMEM((D // steps // 2, LANES), jnp.float32)],
        compiler_params=pltpu.CompilerParams(vmem_limit_bytes=VMEM_LIMIT),
    )(squares, grad_blocks, master, first_moment, second_moment)


def unpack_kernel(block_ref, low_ref, high_ref):
    for pair in range(block_ref.shape[0] // 2):
        lanes = slice(LANES * pair, LANES * (pair + 1))
        first = block_ref[2 * pair].astype(jnp.float32)
        second = block_ref[2 * pair + 1].astype(jnp.float32)
        low_ref[:, lanes] = low_halves(first, second).astype(jnp.bfloat16)
        high_ref[:, lanes] = high_halves(first, second).astype(jnp.bfloat16)


def unpack(blocks):
    peers, middle, _ = blocks.shape
    steps = 4
    half = pl.BlockSpec((middle, peers * HALF // steps), lambda i: (0, i))
    return pl.pallas_call(
        unpack_kernel,
        grid=(steps,),
        in_specs=[pl.BlockSpec((peers // steps, middle, LANES), lambda i: (i, 0, 0))],
        out_specs=[half, half],
        out_shape=[jax.ShapeDtypeStruct((middle, peers * HALF), jnp.bfloat16)] * 2,
        compiler_params=pltpu.CompilerParams(vmem_limit_bytes=VMEM_LIMIT),
    )(blocks)


def shift(array, chips):
    size = lax.axis_size("grp")
    return lax.ppermute(array, "grp", [(i, (i + 2 * chips) % size) for i in range(size)])


def other_core(array):
    return lax.ppermute(array, "grp", [(i, i ^ 1) for i in range(lax.axis_size("grp"))])


def gather_experts(mine, onward):
    after, before = shift(mine, -1), shift(mine, 1)
    far = shift(before if onward > 0 else after, onward)
    by_chip = [mine, after, far, before]
    return [held for near in by_chip for held in (near, other_core(near))]


def place_kernel(halves, slot_ref, *refs):
    held, out_ref, blank_ref, sems = refs[:-3], refs[-3], refs[-2], refs[-1]
    slots, columns = out_ref.shape[0], out_ref.shape[1] // halves
    sources = len(held) // halves
    me = lax.axis_index("grp")

    def copy(source, slot, half):
        target = out_ref.at[slot, pl.ds(half * columns, columns)]
        return pltpu.make_async_copy(source, target, sems.at[slot, half])

    blank_ref[...] = jnp.zeros_like(blank_ref)
    for slot in range(slots):
        expert = slot_ref[slot]
        chips = (expert // 2 - me // 2 + sources // 2) % (sources // 2)
        place = jnp.where(expert < 0, -1, 2 * chips + (expert + me) % 2)
        for half in range(halves):

            @pl.when(place < 0)
            def _():
                copy(blank_ref, slot, half).start()

            for source in range(sources):

                @pl.when(place == source)
                def _():
                    copy(held[half * sources + source], slot, half).start()

    for slot in range(slots):
        for half in range(halves):
            copy(blank_ref, slot, half).wait()


def place(slot_ids, experts):
    slots, halves = slot_ids.shape[0], len(experts)
    columns, rows = experts[0][0].shape
    held = [array for half in experts for array in half]
    return pl.pallas_call(
        functools.partial(place_kernel, halves),
        in_specs=[pl.BlockSpec(memory_space=pltpu.SMEM)] + [pl.BlockSpec(memory_space=pl.ANY)] * len(held),
        out_specs=pl.BlockSpec(memory_space=pl.ANY),
        out_shape=jax.ShapeDtypeStruct((slots, halves * columns, rows), jnp.bfloat16),
        scratch_shapes=[pltpu.VMEM((columns, rows), jnp.bfloat16), pltpu.SemaphoreType.DMA((slots, halves))],
        compiler_params=pltpu.CompilerParams(vmem_limit_bytes=VMEM_LIMIT),
    )(slot_ids, *held)


def total_everywhere(partial):
    for axis in ("grp", "fsdp"):
        size, apart = lax.axis_size(axis), 1
        while apart < size:
            partial += lax.ppermute(partial, axis, [(i, i ^ apart) for i in range(size)])
            apart *= 2
    return partial


def body(gradient, master, first_moment, second_moment, slot_expert):
    entries = lax.axis_size("grp") * master.shape[0] * FF * D
    slot_ids = slot_expert.reshape(-1)
    grad_blocks, squares = pack(jnp.swapaxes(gradient[0], 0, 1))
    grad_here = lax.all_to_all(grad_blocks, "fsdp", 0, 0, tiled=True)
    squares = total_everywhere(squares)
    weights = adam(entries, squares, grad_here, master[0], first_moment[0], second_moment[0])
    columns = lax.all_to_all(weights, "fsdp", 0, 0, tiled=True)
    low, high = unpack(columns)
    rollout = place(slot_ids, [gather_experts(low, 1), gather_experts(high, -1)])
    return jnp.swapaxes(rollout, 1, 2)


def solution(mesh):
    in_specs = (
        P("grp", None, "fsdp"),
        P("grp", "fsdp", None),
        P("grp", "fsdp", None),
        P("grp", "fsdp", None),
        P("grp", None),
    )
    out_specs = P("grp", None, "fsdp")
    return jax.shard_map(body, mesh=mesh, in_specs=in_specs, out_specs=out_specs, check_vma=False)
```

```python
import functools

import jax
import jax.numpy as jnp
from jax import lax
from jax.experimental import pallas as pl
from jax.experimental.pallas import tpu as pltpu
from jax.sharding import PartitionSpec as P

D = 7168
FF = 2048


first_decay = 0.9
second_decay = 0.95
first_bias = 1.0 - 0.9**10
second_bias = 1.0 - 0.95**10
learn_rate = 0.2
shrink = 0.98
epsilon = 1e-08
stabilizer = 1e-06
clip_level = 1.0

LANES = 128
HALF = 64
CHUNKS = 4
EXCHANGES = (("grp", 1, 2), ("grp", 2, 4), ("fsdp", 1, 4), ("fsdp", 4, 4), ("fsdp", 16, 2))
VMEM_LIMIT = 16 * 1024 * 1024


def low_halves(a, b):
    return jnp.concatenate([a[:, :HALF], b[:, :HALF]], axis=1)


def high_halves(a, b):
    return jnp.concatenate([a[:, HALF:], b[:, HALF:]], axis=1)


def pack_kernel(grad_hbm, block_hbm, square_ref, grad_ref, block_ref, in_sems, out_sems):
    steps, columns, rows = in_sems.shape[0], grad_hbm.shape[0], grad_hbm.shape[1]
    middle, width, owners = columns // 2, rows // steps, rows // steps // HALF
    arrive, leave = [], []
    for i in range(steps):
        lanes, blocks = pl.ds(i * width, width), pl.ds(i * owners, owners)
        arrive.append(pltpu.make_async_copy(grad_hbm.at[:, lanes], grad_ref.at[:, lanes], in_sems.at[i]))
        leave.append(pltpu.make_async_copy(block_ref.at[blocks], block_hbm.at[blocks], out_sems.at[i]))
        arrive[i].start()
    squares = jnp.zeros((8, LANES), jnp.float32)
    for i in range(steps):
        arrive[i].wait()
        for pair in range(i * owners // 2, (i + 1) * owners // 2):
            lanes = slice(LANES * pair, LANES * (pair + 1))
            first, second = grad_ref[:middle, lanes], grad_ref[middle:, lanes]
            squares += jnp.sum((first * first + second * second).reshape(-1, 8, LANES), axis=0)
            block_ref[2 * pair] = low_halves(first, second).astype(jnp.bfloat16)
            block_ref[2 * pair + 1] = high_halves(first, second).astype(jnp.bfloat16)
        leave[i].start()
    square_ref[...] = jnp.sum(squares, axis=0, keepdims=True)
    for copy in leave:
        copy.wait()


def pack(grad_columns):
    columns, rows = grad_columns.shape
    steps = 4
    block = (rows // HALF, columns // 2, LANES)
    far = pl.BlockSpec(memory_space=pltpu.HBM)
    return pl.pallas_call(
        pack_kernel,
        in_specs=[far],
        out_specs=[far, pl.BlockSpec(memory_space=pltpu.VMEM)],
        out_shape=[jax.ShapeDtypeStruct(block, jnp.bfloat16), jax.ShapeDtypeStruct((1, LANES), jnp.float32)],
        scratch_shapes=[
            pltpu.VMEM((columns, rows), jnp.float32),
            pltpu.VMEM(block, jnp.bfloat16),
            pltpu.SemaphoreType.DMA((steps,)),
            pltpu.SemaphoreType.DMA((steps,)),
        ],
        compiler_params=pltpu.CompilerParams(vmem_limit_bytes=VMEM_LIMIT),
    )(pltpu.with_memory_space_constraint(grad_columns, pltpu.HBM))


def turn_kernel(grad_ref, master_hbm, first_hbm, second_hbm, turned_ref, master_ref, first_ref, second_ref, flat_ref, sems):
    held = ((master_hbm, master_ref), (first_hbm, first_ref), (second_hbm, second_ref))
    copies = [pltpu.make_async_copy(source, target, sems.at[k]) for k, (source, target) in enumerate(held)]
    for copy in copies:
        copy.start()
    middle, sources = grad_ref.shape[1], grad_ref.shape[0] // CHUNKS
    squares = turned_ref.shape[0] // CHUNKS
    for i in range(CHUNKS):
        for s in range(sources // 2):
            low = grad_ref[sources * i + s].astype(jnp.float32)
            high = grad_ref[sources * i + sources // 2 + s].astype(jnp.float32)
            at = 2 * middle * s
            flat_ref[at : at + middle] = low_halves(low, high)
            flat_ref[at + middle : at + 2 * middle] = high_halves(low, high)
        for j in range(squares):
            turned_ref[squares * i + j] = flat_ref[LANES * j : LANES * (j + 1)].T
    for copy in copies:
        copy.wait()


def turn(grad_blocks, *states):
    near, far = pl.BlockSpec(memory_space=pltpu.VMEM), pl.BlockSpec(memory_space=pltpu.HBM)
    state = jax.ShapeDtypeStruct(states[0].shape, jnp.float32)
    return pl.pallas_call(
        turn_kernel,
        in_specs=[near, far, far, far],
        out_specs=[near] * 4,
        out_shape=[jax.ShapeDtypeStruct((D // LANES // 2, LANES, LANES), jnp.float32)] + [state] * 3,
        scratch_shapes=[pltpu.VMEM((D // CHUNKS // 2, LANES), jnp.float32), pltpu.SemaphoreType.DMA((3,))],
        compiler_params=pltpu.CompilerParams(vmem_limit_bytes=VMEM_LIMIT),
    )(grad_blocks, *[pltpu.with_memory_space_constraint(a, pltpu.HBM) for a in states])


def adam_weights(gradient, master, first_moment, second_moment, factor):
    scaled = factor * gradient
    first_new = first_decay * first_moment + (1.0 - first_decay) * scaled
    second_new = second_decay * second_moment + (1.0 - second_decay) * scaled * scaled
    update = first_new / first_bias / (jnp.sqrt(second_new / second_bias) + epsilon)
    return shrink * master - learn_rate * update


def adam_kernel(entries, squares_ref, turned_ref, master_ref, first_ref, second_ref, out_ref, flat_ref):
    square_total = jnp.sum(squares_ref[...])
    factor = jnp.minimum(1.0, clip_level / jnp.sqrt(square_total / entries + stabilizer))
    sources, middle = out_ref.shape[0] // CHUNKS, out_ref.shape[1]
    width, squares = D // CHUNKS, turned_ref.shape[0] // CHUNKS
    for i in range(CHUNKS):
        for j in range(squares):
            at = width * i + LANES * j
            beyond = at + width // 2
            both = lambda ref: jnp.concatenate([ref[:, at : at + LANES], ref[:, beyond : beyond + LANES]], axis=0)
            gradient = turned_ref[squares * i + j]
            weights = adam_weights(gradient, both(master_ref), both(first_ref), both(second_ref), factor)
            flat_ref[LANES * j : LANES * (j + 1)] = weights.T
        for s in range(sources // 2):
            at = 2 * middle * s
            first, second = flat_ref[at : at + middle], flat_ref[at + middle : at + 2 * middle]
            out_ref[sources * i + s] = low_halves(first, second).astype(jnp.bfloat16)
            out_ref[sources * i + sources // 2 + s] = high_halves(first, second).astype(jnp.bfloat16)


def adam(entries, squares, turned, *states):
    near = pl.BlockSpec(memory_space=pltpu.VMEM)
    rows, columns = states[0].shape
    return pl.pallas_call(
        functools.partial(adam_kernel, entries),
        in_specs=[near] * 5,
        out_specs=near,
        out_shape=jax.ShapeDtypeStruct((FF // rows, columns * rows // FF // 2, LANES), jnp.bfloat16),
        scratch_shapes=[pltpu.VMEM((D // CHUNKS // 2, LANES), jnp.float32)],
        compiler_params=pltpu.CompilerParams(vmem_limit_bytes=VMEM_LIMIT),
    )(squares, turned, *states)


def unpack_kernel(block_ref, low_ref, high_ref):
    for pair in range(block_ref.shape[0] // 2):
        lanes = slice(LANES * pair, LANES * (pair + 1))
        first = block_ref[2 * pair].astype(jnp.float32)
        second = block_ref[2 * pair + 1].astype(jnp.float32)
        low_ref[:, lanes] = low_halves(first, second).astype(jnp.bfloat16)
        high_ref[:, lanes] = high_halves(first, second).astype(jnp.bfloat16)


def unpack(blocks):
    peers, middle, _ = blocks.shape
    steps = 4
    half = pl.BlockSpec((middle, peers * HALF // steps), lambda i: (0, i))
    return pl.pallas_call(
        unpack_kernel,
        grid=(steps,),
        in_specs=[pl.BlockSpec((peers // steps, middle, LANES), lambda i: (i, 0, 0))],
        out_specs=[half, half],
        out_shape=[jax.ShapeDtypeStruct((middle, peers * HALF), jnp.bfloat16)] * 2,
        compiler_params=pltpu.CompilerParams(vmem_limit_bytes=VMEM_LIMIT),
    )(blocks)


def shift(array, chips):
    size = lax.axis_size("grp")
    return lax.ppermute(array, "grp", [(i, (i + 2 * chips) % size) for i in range(size)])


def other_core(array):
    return lax.ppermute(array, "grp", [(i, i ^ 1) for i in range(lax.axis_size("grp"))])


def gather_experts(mine, onward):
    after, before = shift(mine, -1), shift(mine, 1)
    far = shift(before if onward > 0 else after, onward)
    by_chip = [mine, after, far, before]
    return [held for near in by_chip for held in (near, other_core(near))]


def place_kernel(halves, slot_ref, *refs):
    held, out_ref, blank_ref, sems = refs[:-3], refs[-3], refs[-2], refs[-1]
    slots, columns = out_ref.shape[0], out_ref.shape[1] // halves
    sources = len(held) // halves
    me = lax.axis_index("grp")

    def copy(source, slot, half):
        target = out_ref.at[slot, pl.ds(half * columns, columns)]
        return pltpu.make_async_copy(source, target, sems.at[slot, half])

    blank_ref[...] = jnp.zeros_like(blank_ref)
    for slot in range(slots):
        expert = slot_ref[slot]
        chips = (expert // 2 - me // 2 + sources // 2) % (sources // 2)
        place = jnp.where(expert < 0, -1, 2 * chips + (expert + me) % 2)
        for half in range(halves):

            @pl.when(place < 0)
            def _():
                copy(blank_ref, slot, half).start()

            for source in range(sources):

                @pl.when(place == source)
                def _():
                    copy(held[half * sources + source], slot, half).start()

    for slot in range(slots):
        for half in range(halves):
            copy(blank_ref, slot, half).wait()


def place(slot_ids, experts):
    slots, halves = slot_ids.shape[0], len(experts)
    columns, rows = experts[0][0].shape
    held = [array for half in experts for array in half]
    return pl.pallas_call(
        functools.partial(place_kernel, halves),
        in_specs=[pl.BlockSpec(memory_space=pltpu.SMEM)] + [pl.BlockSpec(memory_space=pl.ANY)] * len(held),
        out_specs=pl.BlockSpec(memory_space=pl.ANY),
        out_shape=jax.ShapeDtypeStruct((slots, halves * columns, rows), jnp.bfloat16),
        scratch_shapes=[pltpu.VMEM((columns, rows), jnp.bfloat16), pltpu.SemaphoreType.DMA((slots, halves))],
        compiler_params=pltpu.CompilerParams(vmem_limit_bytes=VMEM_LIMIT),
    )(slot_ids, *held)


def total_over(partial, axis, apart, radix):
    size = lax.axis_size(axis)
    others = [lax.ppermute(partial, axis, [(i, i ^ (apart * k)) for i in range(size)]) for k in range(1, radix)]
    return sum(others, partial)


def body(gradient, master, first_moment, second_moment, slot_expert):
    entries = lax.axis_size("grp") * master.shape[0] * FF * D
    slot_ids = slot_expert.reshape(-1)
    grad_blocks, squares = pack(jnp.swapaxes(gradient[0], 0, 1))
    grad_here = lax.all_to_all(grad_blocks, "fsdp", 0, 0, tiled=True)
    for axis, apart, radix in EXCHANGES[:-1]:
        squares = total_over(squares, axis, apart, radix)
    turned, *states = turn(grad_here, master[0], first_moment[0], second_moment[0])
    axis, apart, _ = EXCHANGES[-1]
    others = lax.ppermute(squares, axis, [(i, i ^ apart) for i in range(lax.axis_size(axis))])
    others, turned = lax.optimization_barrier((others, turned))
    squares = squares + others
    weights = adam(entries, squares, turned, *states)
    columns = lax.all_to_all(weights, "fsdp", 0, 0, tiled=True)
    low, high = unpack(columns)
    rollout = place(slot_ids, [gather_experts(low, 1), gather_experts(high, -1)])
    return jnp.swapaxes(rollout, 1, 2)


def solution(mesh):
    in_specs = (
        P("grp", None, "fsdp"),
        P("grp", "fsdp", None),
        P("grp", "fsdp", None),
        P("grp", "fsdp", None),
        P("grp", None),
    )
    out_specs = P("grp", None, "fsdp")
    return jax.shard_map(body, mesh=mesh, in_specs=in_specs, out_specs=out_specs, check_vma=False)
```

```python
import functools

import jax
import jax.numpy as jnp
from jax import lax
from jax.experimental import pallas as pl
from jax.experimental.pallas import tpu as pltpu
from jax.sharding import PartitionSpec as P

D = 7168
FF = 2048


first_decay = 0.9
second_decay = 0.95
first_bias = 1.0 - 0.9**10
second_bias = 1.0 - 0.95**10
learn_rate = 0.2
shrink = 0.98
epsilon = 1e-08
stabilizer = 1e-06
clip_level = 1.0

LANES = 128
HALF = 64
CHUNKS = 4
FIRST = (-1, 0, 1, 2, 3, 6, 7)
SECOND = (4, 5)
COST = 2
EXCHANGES = (("grp", 1, 2), ("grp", 2, 4), ("fsdp", 1, 4), ("fsdp", 4, 4), ("fsdp", 16, 2))
VMEM_LIMIT = 16 * 1024 * 1024


def low_halves(a, b):
    return jnp.concatenate([a[:, :HALF], b[:, :HALF]], axis=1)


def high_halves(a, b):
    return jnp.concatenate([a[:, HALF:], b[:, HALF:]], axis=1)


def pack_kernel(grad_hbm, block_hbm, square_ref, grad_ref, block_ref, in_sems, out_sems):
    steps, columns, rows = in_sems.shape[0], grad_hbm.shape[0], grad_hbm.shape[1]
    middle, width, owners = columns // 2, rows // steps, rows // steps // HALF
    arrive, leave = [], []
    for i in range(steps):
        lanes, blocks = pl.ds(i * width, width), pl.ds(i * owners, owners)
        arrive.append(pltpu.make_async_copy(grad_hbm.at[:, lanes], grad_ref.at[:, lanes], in_sems.at[i]))
        leave.append(pltpu.make_async_copy(block_ref.at[blocks], block_hbm.at[blocks], out_sems.at[i]))
        arrive[i].start()
    squares = jnp.zeros((8, LANES), jnp.float32)
    for i in range(steps):
        arrive[i].wait()
        for pair in range(i * owners // 2, (i + 1) * owners // 2):
            lanes = slice(LANES * pair, LANES * (pair + 1))
            first, second = grad_ref[:middle, lanes], grad_ref[middle:, lanes]
            squares += jnp.sum((first * first + second * second).reshape(-1, 8, LANES), axis=0)
            block_ref[2 * pair] = low_halves(first, second).astype(jnp.bfloat16)
            block_ref[2 * pair + 1] = high_halves(first, second).astype(jnp.bfloat16)
        leave[i].start()
    square_ref[...] = jnp.sum(squares, axis=0, keepdims=True)
    for copy in leave:
        copy.wait()


def pack(grad_columns):
    columns, rows = grad_columns.shape
    steps = 4
    block = (rows // HALF, columns // 2, LANES)
    far = pl.BlockSpec(memory_space=pltpu.HBM)
    return pl.pallas_call(
        pack_kernel,
        in_specs=[far],
        out_specs=[far, pl.BlockSpec(memory_space=pltpu.VMEM)],
        out_shape=[jax.ShapeDtypeStruct(block, jnp.bfloat16), jax.ShapeDtypeStruct((1, LANES), jnp.float32)],
        scratch_shapes=[
            pltpu.VMEM((columns, rows), jnp.float32),
            pltpu.VMEM(block, jnp.bfloat16),
            pltpu.SemaphoreType.DMA((steps,)),
            pltpu.SemaphoreType.DMA((steps,)),
        ],
        compiler_params=pltpu.CompilerParams(vmem_limit_bytes=VMEM_LIMIT),
    )(pltpu.with_memory_space_constraint(grad_columns, pltpu.HBM))


def turn_kernel(grad_ref, master_hbm, first_hbm, second_hbm, turned_ref, master_ref, first_ref, second_ref, flat_ref, sems):
    held = ((master_hbm, master_ref), (first_hbm, first_ref), (second_hbm, second_ref))
    copies = [pltpu.make_async_copy(source, target, sems.at[k]) for k, (source, target) in enumerate(held)]
    for copy in copies:
        copy.start()
    middle, sources = grad_ref.shape[1], grad_ref.shape[0] // CHUNKS
    squares = turned_ref.shape[0] // CHUNKS
    for i in range(CHUNKS):
        for s in range(sources // 2):
            low = grad_ref[sources * i + s].astype(jnp.float32)
            high = grad_ref[sources * i + sources // 2 + s].astype(jnp.float32)
            at = 2 * middle * s
            flat_ref[at : at + middle] = low_halves(low, high)
            flat_ref[at + middle : at + 2 * middle] = high_halves(low, high)
        for j in range(squares):
            turned_ref[squares * i + j] = flat_ref[LANES * j : LANES * (j + 1)].T
    for copy in copies:
        copy.wait()


def turn(grad_blocks, *states):
    near, far = pl.BlockSpec(memory_space=pltpu.VMEM), pl.BlockSpec(memory_space=pltpu.HBM)
    state = jax.ShapeDtypeStruct(states[0].shape, jnp.float32)
    return pl.pallas_call(
        turn_kernel,
        in_specs=[near, far, far, far],
        out_specs=[near] * 4,
        out_shape=[jax.ShapeDtypeStruct((D // LANES // 2, LANES, LANES), jnp.float32)] + [state] * 3,
        scratch_shapes=[pltpu.VMEM((D // CHUNKS // 2, LANES), jnp.float32), pltpu.SemaphoreType.DMA((3,))],
        compiler_params=pltpu.CompilerParams(vmem_limit_bytes=VMEM_LIMIT),
    )(grad_blocks, *[pltpu.with_memory_space_constraint(a, pltpu.HBM) for a in states])


def adam_weights(gradient, master, first_moment, second_moment, factor):
    scaled = factor * gradient
    first_new = first_decay * first_moment + (1.0 - first_decay) * scaled
    second_new = second_decay * second_moment + (1.0 - second_decay) * scaled * scaled
    update = first_new / first_bias / (jnp.sqrt(second_new / second_bias) + epsilon)
    return shrink * master - learn_rate * update


def adam_kernel(entries, squares_ref, turned_ref, master_ref, first_ref, second_ref, out_ref, flat_ref):
    square_total = jnp.sum(squares_ref[...])
    factor = jnp.minimum(1.0, clip_level / jnp.sqrt(square_total / entries + stabilizer))
    sources, middle = out_ref.shape[0] // CHUNKS, out_ref.shape[1]
    width, squares = D // CHUNKS, turned_ref.shape[0] // CHUNKS
    for i in range(CHUNKS):
        for j in range(squares):
            at = width * i + LANES * j
            beyond = at + width // 2
            both = lambda ref: jnp.concatenate([ref[:, at : at + LANES], ref[:, beyond : beyond + LANES]], axis=0)
            gradient = turned_ref[squares * i + j]
            weights = adam_weights(gradient, both(master_ref), both(first_ref), both(second_ref), factor)
            flat_ref[LANES * j : LANES * (j + 1)] = weights.T
        for s in range(sources // 2):
            at = 2 * middle * s
            first, second = flat_ref[at : at + middle], flat_ref[at + middle : at + 2 * middle]
            out_ref[sources * i + s] = low_halves(first, second).astype(jnp.bfloat16)
            out_ref[sources * i + sources // 2 + s] = high_halves(first, second).astype(jnp.bfloat16)


def adam(entries, squares, turned, *states):
    near = pl.BlockSpec(memory_space=pltpu.VMEM)
    rows, columns = states[0].shape
    return pl.pallas_call(
        functools.partial(adam_kernel, entries),
        in_specs=[near] * 5,
        out_specs=near,
        out_shape=jax.ShapeDtypeStruct((FF // rows, columns * rows // FF // 2, LANES), jnp.bfloat16),
        scratch_shapes=[pltpu.VMEM((D // CHUNKS // 2, LANES), jnp.float32)],
        compiler_params=pltpu.CompilerParams(vmem_limit_bytes=VMEM_LIMIT),
    )(squares, turned, *states)


def unpack_kernel(block_ref, low_ref, high_ref):
    for pair in range(block_ref.shape[0] // 2):
        lanes = slice(LANES * pair, LANES * (pair + 1))
        first = block_ref[2 * pair].astype(jnp.float32)
        second = block_ref[2 * pair + 1].astype(jnp.float32)
        low_ref[:, lanes] = low_halves(first, second).astype(jnp.bfloat16)
        high_ref[:, lanes] = high_halves(first, second).astype(jnp.bfloat16)


def unpack(blocks):
    peers, middle, _ = blocks.shape
    steps = 4
    half = pl.BlockSpec((middle, peers * HALF // steps), lambda i: (0, i))
    return pl.pallas_call(
        unpack_kernel,
        grid=(steps,),
        in_specs=[pl.BlockSpec((peers // steps, middle, LANES), lambda i: (i, 0, 0))],
        out_specs=[half, half],
        out_shape=[jax.ShapeDtypeStruct((middle, peers * HALF), jnp.bfloat16)] * 2,
        compiler_params=pltpu.CompilerParams(vmem_limit_bytes=VMEM_LIMIT),
    )(blocks)


def shift(array, chips):
    size = lax.axis_size("grp")
    return lax.ppermute(array, "grp", [(i, (i + 2 * chips) % size) for i in range(size)])


def other_core(array):
    return lax.ppermute(array, "grp", [(i, i ^ 1) for i in range(lax.axis_size("grp"))])


def place_kernel(keys, halves, slot_ref, *refs):
    held, out_ref, blank_ref, sems = refs[: len(keys) * halves], refs[-3], refs[-2], refs[-1]
    slots, columns = out_ref.shape[0], out_ref.shape[1] // halves
    me, chips = lax.axis_index("grp"), lax.axis_size("grp") // 2

    def copy(source, slot, half):
        target = out_ref.at[slot, pl.ds(half * columns, columns)]
        return pltpu.make_async_copy(source, target, sems.at[slot, half])

    if -1 in keys:
        blank_ref[...] = jnp.zeros_like(blank_ref)
    places = []
    for slot in range(slots):
        expert = slot_ref[slot]
        apart = (expert // 2 - me // 2 + chips) % chips
        places.append(jnp.where(expert < 0, -1, 2 * apart + (expert + me) % 2))
    for act in ("start", "wait"):
        for slot in range(slots):
            for at, key in enumerate(keys):

                @pl.when(places[slot] == key)
                def _():
                    for half in range(halves):
                        source = blank_ref if key < 0 else held[half * len(keys) + at]
                        getattr(copy(source, slot, half), act)()


def place(slot_ids, keys, experts, rollout=None):
    slots, halves = slot_ids.shape[0], len(experts)
    columns, rows = experts[0][keys[-1]].shape
    held = [half[key] if key >= 0 else half[keys[-1]] for half in experts for key in keys]
    extra = [] if rollout is None else [rollout]
    far = pl.BlockSpec(memory_space=pl.ANY)
    size = len(keys) * halves * columns * rows
    return pl.pallas_call(
        functools.partial(place_kernel, keys, halves),
        in_specs=[pl.BlockSpec(memory_space=pltpu.SMEM)] + [far] * (len(held) + len(extra)),
        out_specs=far,
        out_shape=jax.ShapeDtypeStruct((slots, halves * columns, rows), jnp.bfloat16),
        scratch_shapes=[pltpu.VMEM((columns, rows), jnp.bfloat16), pltpu.SemaphoreType.DMA((slots, halves))],
        input_output_aliases={1 + len(held): 0} if extra else {},
        cost_estimate=pl.CostEstimate(flops=0, bytes_accessed=COST * size, transcendentals=0),
        compiler_params=pltpu.CompilerParams(vmem_limit_bytes=VMEM_LIMIT),
    )(slot_ids, *held, *extra)


def total_over(partial, axis, apart, radix):
    size = lax.axis_size(axis)
    others = [lax.ppermute(partial, axis, [(i, i ^ (apart * k)) for i in range(size)]) for k in range(1, radix)]
    return sum(others, partial)


def body(gradient, master, first_moment, second_moment, slot_expert):
    entries = lax.axis_size("grp") * master.shape[0] * FF * D
    slot_ids = slot_expert.reshape(-1)
    grad_blocks, squares = pack(jnp.swapaxes(gradient[0], 0, 1))
    grad_here = lax.all_to_all(grad_blocks, "fsdp", 0, 0, tiled=True)
    for axis, apart, radix in EXCHANGES[:-1]:
        squares = total_over(squares, axis, apart, radix)
    turned, *states = turn(grad_here, master[0], first_moment[0], second_moment[0])
    axis, apart, _ = EXCHANGES[-1]
    others = lax.ppermute(squares, axis, [(i, i ^ apart) for i in range(lax.axis_size(axis))])
    others, turned = lax.optimization_barrier((others, turned))
    squares = squares + others
    weights = adam(entries, squares, turned, *states)
    columns = lax.all_to_all(weights, "fsdp", 0, 0, tiled=True)
    low, high = unpack(columns)
    halves = [{0: low}, {0: high}]
    for half, onward in zip(halves, (1, -1)):
        half[2], half[6] = shift(half[0], -1), shift(half[0], 1)
        half[4] = shift(half[6] if onward > 0 else half[2], onward)
        half[1], half[3], half[7] = other_core(half[0]), other_core(half[2]), other_core(half[6])
    rollout = place(slot_ids, FIRST, halves)
    for half in halves:
        half[5] = other_core(half[4])
    rollout = place(slot_ids, SECOND, halves, rollout)
    return jnp.swapaxes(rollout, 1, 2)


def solution(mesh):
    in_specs = (
        P("grp", None, "fsdp"),
        P("grp", "fsdp", None),
        P("grp", "fsdp", None),
        P("grp", "fsdp", None),
        P("grp", None),
    )
    out_specs = P("grp", None, "fsdp")
    return jax.shard_map(body, mesh=mesh, in_specs=in_specs, out_specs=out_specs, check_vma=False)
```

```python
import functools

import jax
import jax.numpy as jnp
from jax import lax
from jax.experimental import pallas as pl
from jax.experimental.pallas import tpu as pltpu
from jax.sharding import PartitionSpec as P

D = 7168
FF = 2048


first_decay = 0.9
second_decay = 0.95
first_bias = 1.0 - 0.9**10
second_bias = 1.0 - 0.95**10
learn_rate = 0.2
shrink = 0.98
epsilon = 1e-08
stabilizer = 1e-06
clip_level = 1.0

LANES = 128
HALF = 64
CHUNKS = 4
FIRST = (-1, 0, 1, 2, 3, 6, 7)
SECOND = (4, 5)
COST = 2
EXCHANGES = (("grp", (1,)), ("grp", (2,)), ("grp", (6,)), ("fsdp", (1,)), ("fsdp", (3,)), ("fsdp", (4, 8, 12)), ("fsdp", (28,)))
VMEM_LIMIT = 16 * 1024 * 1024


def low_halves(a, b):
    return jnp.concatenate([a[:, :HALF], b[:, :HALF]], axis=1)


def high_halves(a, b):
    return jnp.concatenate([a[:, HALF:], b[:, HALF:]], axis=1)


def pack_kernel(grad_hbm, block_hbm, square_ref, grad_ref, block_ref, in_sems, out_sems):
    steps, columns, rows = in_sems.shape[0], grad_hbm.shape[0], grad_hbm.shape[1]
    middle, width, owners = columns // 2, rows // steps, rows // steps // HALF
    arrive, leave = [], []
    for i in range(steps):
        lanes, blocks = pl.ds(i * width, width), pl.ds(i * owners, owners)
        arrive.append(pltpu.make_async_copy(grad_hbm.at[:, lanes], grad_ref.at[:, lanes], in_sems.at[i]))
        leave.append(pltpu.make_async_copy(block_ref.at[blocks], block_hbm.at[blocks], out_sems.at[i]))
        arrive[i].start()
    squares = jnp.zeros((8, LANES), jnp.float32)
    for i in range(steps):
        arrive[i].wait()
        for pair in range(i * owners // 2, (i + 1) * owners // 2):
            lanes = slice(LANES * pair, LANES * (pair + 1))
            first, second = grad_ref[:middle, lanes], grad_ref[middle:, lanes]
            squares += jnp.sum((first * first + second * second).reshape(-1, 8, LANES), axis=0)
            block_ref[2 * pair] = low_halves(first, second).astype(jnp.bfloat16)
            block_ref[2 * pair + 1] = high_halves(first, second).astype(jnp.bfloat16)
        leave[i].start()
    square_ref[...] = jnp.sum(squares, axis=0, keepdims=True)
    for copy in leave:
        copy.wait()


def pack(grad_columns):
    columns, rows = grad_columns.shape
    steps = 4
    block = (rows // HALF, columns // 2, LANES)
    far = pl.BlockSpec(memory_space=pltpu.HBM)
    return pl.pallas_call(
        pack_kernel,
        in_specs=[far],
        out_specs=[far, pl.BlockSpec(memory_space=pltpu.VMEM)],
        out_shape=[jax.ShapeDtypeStruct(block, jnp.bfloat16), jax.ShapeDtypeStruct((1, LANES), jnp.float32)],
        scratch_shapes=[
            pltpu.VMEM((columns, rows), jnp.float32),
            pltpu.VMEM(block, jnp.bfloat16),
            pltpu.SemaphoreType.DMA((steps,)),
            pltpu.SemaphoreType.DMA((steps,)),
        ],
        compiler_params=pltpu.CompilerParams(vmem_limit_bytes=VMEM_LIMIT),
    )(pltpu.with_memory_space_constraint(grad_columns, pltpu.HBM))


def turn_kernel(grad_ref, master_hbm, first_hbm, second_hbm, turned_ref, master_ref, first_ref, second_ref, flat_ref, sems):
    held = ((master_hbm, master_ref), (first_hbm, first_ref), (second_hbm, second_ref))
    copies = [pltpu.make_async_copy(source, target, sems.at[k]) for k, (source, target) in enumerate(held)]
    for copy in copies:
        copy.start()
    middle, sources = grad_ref.shape[1], grad_ref.shape[0] // CHUNKS
    squares = turned_ref.shape[0] // CHUNKS
    for i in range(CHUNKS):
        for s in range(sources // 2):
            low = grad_ref[sources * i + s].astype(jnp.float32)
            high = grad_ref[sources * i + sources // 2 + s].astype(jnp.float32)
            at = 2 * middle * s
            flat_ref[at : at + middle] = low_halves(low, high)
            flat_ref[at + middle : at + 2 * middle] = high_halves(low, high)
        for j in range(squares):
            turned_ref[squares * i + j] = flat_ref[LANES * j : LANES * (j + 1)].T
    for copy in copies:
        copy.wait()


def turn(grad_blocks, *states):
    near, far = pl.BlockSpec(memory_space=pltpu.VMEM), pl.BlockSpec(memory_space=pltpu.HBM)
    state = jax.ShapeDtypeStruct(states[0].shape, jnp.float32)
    return pl.pallas_call(
        turn_kernel,
        in_specs=[near, far, far, far],
        out_specs=[near] * 4,
        out_shape=[jax.ShapeDtypeStruct((D // LANES // 2, LANES, LANES), jnp.float32)] + [state] * 3,
        scratch_shapes=[pltpu.VMEM((D // CHUNKS // 2, LANES), jnp.float32), pltpu.SemaphoreType.DMA((3,))],
        compiler_params=pltpu.CompilerParams(vmem_limit_bytes=VMEM_LIMIT),
    )(grad_blocks, *[pltpu.with_memory_space_constraint(a, pltpu.HBM) for a in states])


def adam_weights(gradient, master, first_moment, second_moment, factor):
    scaled = factor * gradient
    first_new = first_decay * first_moment + (1.0 - first_decay) * scaled
    second_new = second_decay * second_moment + (1.0 - second_decay) * scaled * scaled
    update = first_new / first_bias / (jnp.sqrt(second_new / second_bias) + epsilon)
    return shrink * master - learn_rate * update


def adam_kernel(entries, squares_ref, turned_ref, master_ref, first_ref, second_ref, out_ref, flat_ref):
    square_total = jnp.sum(squares_ref[...])
    factor = jnp.minimum(1.0, clip_level / jnp.sqrt(square_total / entries + stabilizer))
    sources, middle = out_ref.shape[0] // CHUNKS, out_ref.shape[1]
    width, squares = D // CHUNKS, turned_ref.shape[0] // CHUNKS
    for i in range(CHUNKS):
        for j in range(squares):
            at = width * i + LANES * j
            beyond = at + width // 2
            both = lambda ref: jnp.concatenate([ref[:, at : at + LANES], ref[:, beyond : beyond + LANES]], axis=0)
            gradient = turned_ref[squares * i + j]
            weights = adam_weights(gradient, both(master_ref), both(first_ref), both(second_ref), factor)
            flat_ref[LANES * j : LANES * (j + 1)] = weights.T
        for s in range(sources // 2):
            at = 2 * middle * s
            first, second = flat_ref[at : at + middle], flat_ref[at + middle : at + 2 * middle]
            out_ref[sources * i + s] = low_halves(first, second).astype(jnp.bfloat16)
            out_ref[sources * i + sources // 2 + s] = high_halves(first, second).astype(jnp.bfloat16)


def adam(entries, squares, turned, *states):
    near = pl.BlockSpec(memory_space=pltpu.VMEM)
    rows, columns = states[0].shape
    return pl.pallas_call(
        functools.partial(adam_kernel, entries),
        in_specs=[near] * 5,
        out_specs=near,
        out_shape=jax.ShapeDtypeStruct((FF // rows, columns * rows // FF // 2, LANES), jnp.bfloat16),
        scratch_shapes=[pltpu.VMEM((D // CHUNKS // 2, LANES), jnp.float32)],
        compiler_params=pltpu.CompilerParams(vmem_limit_bytes=VMEM_LIMIT),
    )(squares, turned, *states)


def unpack_kernel(block_ref, low_ref, high_ref):
    for pair in range(block_ref.shape[0] // 2):
        lanes = slice(LANES * pair, LANES * (pair + 1))
        first = block_ref[2 * pair].astype(jnp.float32)
        second = block_ref[2 * pair + 1].astype(jnp.float32)
        low_ref[:, lanes] = low_halves(first, second).astype(jnp.bfloat16)
        high_ref[:, lanes] = high_halves(first, second).astype(jnp.bfloat16)


def unpack(blocks):
    peers, middle, _ = blocks.shape
    steps = 4
    half = pl.BlockSpec((middle, peers * HALF // steps), lambda i: (0, i))
    return pl.pallas_call(
        unpack_kernel,
        grid=(steps,),
        in_specs=[pl.BlockSpec((peers // steps, middle, LANES), lambda i: (i, 0, 0))],
        out_specs=[half, half],
        out_shape=[jax.ShapeDtypeStruct((middle, peers * HALF), jnp.bfloat16)] * 2,
        compiler_params=pltpu.CompilerParams(vmem_limit_bytes=VMEM_LIMIT),
    )(blocks)


def shift(array, chips):
    size = lax.axis_size("grp")
    return lax.ppermute(array, "grp", [(i, (i + 2 * chips) % size) for i in range(size)])


def other_core(array):
    return lax.ppermute(array, "grp", [(i, i ^ 1) for i in range(lax.axis_size("grp"))])


def place_kernel(keys, halves, slot_ref, *refs):
    held, out_ref, blank_ref, sems = refs[: len(keys) * halves], refs[-3], refs[-2], refs[-1]
    slots, columns = out_ref.shape[0], out_ref.shape[1] // halves
    me, chips = lax.axis_index("grp"), lax.axis_size("grp") // 2

    def copy(source, slot, half):
        target = out_ref.at[slot, pl.ds(half * columns, columns)]
        return pltpu.make_async_copy(source, target, sems.at[slot, half])

    if -1 in keys:
        blank_ref[...] = jnp.zeros_like(blank_ref)
    places = []
    for slot in range(slots):
        expert = slot_ref[slot]
        apart = (expert // 2 - me // 2 + chips) % chips
        places.append(jnp.where(expert < 0, -1, 2 * apart + (expert + me) % 2))
    for act in ("start", "wait"):
        for slot in range(slots):
            for at, key in enumerate(keys):

                @pl.when(places[slot] == key)
                def _():
                    for half in range(halves):
                        source = blank_ref if key < 0 else held[half * len(keys) + at]
                        getattr(copy(source, slot, half), act)()


def place(slot_ids, keys, experts, rollout=None):
    slots, halves = slot_ids.shape[0], len(experts)
    columns, rows = experts[0][keys[-1]].shape
    held = [half[key] if key >= 0 else half[keys[-1]] for half in experts for key in keys]
    extra = [] if rollout is None else [rollout]
    far = pl.BlockSpec(memory_space=pl.ANY)
    size = len(keys) * halves * columns * rows
    return pl.pallas_call(
        functools.partial(place_kernel, keys, halves),
        in_specs=[pl.BlockSpec(memory_space=pltpu.SMEM)] + [far] * (len(held) + len(extra)),
        out_specs=far,
        out_shape=jax.ShapeDtypeStruct((slots, halves * columns, rows), jnp.bfloat16),
        scratch_shapes=[pltpu.VMEM((columns, rows), jnp.bfloat16), pltpu.SemaphoreType.DMA((slots, halves))],
        input_output_aliases={1 + len(held): 0} if extra else {},
        cost_estimate=pl.CostEstimate(flops=0, bytes_accessed=COST * size, transcendentals=0),
        compiler_params=pltpu.CompilerParams(vmem_limit_bytes=VMEM_LIMIT),
    )(slot_ids, *held, *extra)


def from_others(partial, axis, masks):
    size = lax.axis_size(axis)
    return [lax.ppermute(partial, axis, [(i, i ^ mask) for i in range(size)]) for mask in masks]


def body(gradient, master, first_moment, second_moment, slot_expert):
    entries = lax.axis_size("grp") * master.shape[0] * FF * D
    slot_ids = slot_expert.reshape(-1)
    grad_blocks, squares = pack(jnp.swapaxes(gradient[0], 0, 1))
    grad_here = lax.all_to_all(grad_blocks, "fsdp", 0, 0, tiled=True)
    for axis, masks in EXCHANGES[:-1]:
        squares = sum(from_others(squares, axis, masks), squares)
    turned, *states = turn(grad_here, master[0], first_moment[0], second_moment[0])
    others, turned = lax.optimization_barrier((from_others(squares, *EXCHANGES[-1]), turned))
    squares = sum(others, squares)
    weights = adam(entries, squares, turned, *states)
    columns = lax.all_to_all(weights, "fsdp", 0, 0, tiled=True)
    low, high = unpack(columns)
    halves = [{0: low}, {0: high}]
    for half, onward in zip(halves, (1, -1)):
        half[2], half[6] = shift(half[0], -1), shift(half[0], 1)
        half[4] = shift(half[6] if onward > 0 else half[2], onward)
        half[1], half[3], half[7] = other_core(half[0]), other_core(half[2]), other_core(half[6])
    rollout = place(slot_ids, FIRST, halves)
    for half in halves:
        half[5] = other_core(half[4])
    rollout = place(slot_ids, SECOND, halves, rollout)
    return jnp.swapaxes(rollout, 1, 2)


def solution(mesh):
    in_specs = (
        P("grp", None, "fsdp"),
        P("grp", "fsdp", None),
        P("grp", "fsdp", None),
        P("grp", "fsdp", None),
        P("grp", None),
    )
    out_specs = P("grp", None, "fsdp")
    return jax.shard_map(body, mesh=mesh, in_specs=in_specs, out_specs=out_specs, check_vma=False)
```

```python
import functools

import jax
import jax.numpy as jnp
from jax import lax
from jax.experimental import pallas as pl
from jax.experimental.pallas import tpu as pltpu
from jax.sharding import PartitionSpec as P

D = 7168
FF = 2048


first_decay = 0.9
second_decay = 0.95
first_bias = 1.0 - 0.9**10
second_bias = 1.0 - 0.95**10
learn_rate = 0.2
shrink = 0.98
epsilon = 1e-08
stabilizer = 1e-06
clip_level = 1.0

LANES = 128
HALF = 64
CHUNKS = 4
FIRST = (-1, 0, 1, 2, 3, 6, 7)
SECOND = (4, 5)
COST = 2
EXCHANGES = (("grp", (1,)), ("grp", (2,)), ("grp", (6,)), ("fsdp", (1,)), ("fsdp", (3,)), ("fsdp", (4, 28, 24)), ("fsdp", (8,)))
VMEM_LIMIT = 16 * 1024 * 1024


def low_halves(a, b):
    return jnp.concatenate([a[:, :HALF], b[:, :HALF]], axis=1)


def high_halves(a, b):
    return jnp.concatenate([a[:, HALF:], b[:, HALF:]], axis=1)


def pack_kernel(grad_hbm, block_hbm, square_ref, grad_ref, block_ref, in_sems, out_sems):
    steps, columns, rows = in_sems.shape[0], grad_hbm.shape[0], grad_hbm.shape[1]
    middle, width, owners = columns // 2, rows // steps, rows // steps // HALF
    arrive, leave = [], []
    for i in range(steps):
        lanes, blocks = pl.ds(i * width, width), pl.ds(i * owners, owners)
        arrive.append(pltpu.make_async_copy(grad_hbm.at[:, lanes], grad_ref.at[:, lanes], in_sems.at[i]))
        leave.append(pltpu.make_async_copy(block_ref.at[blocks], block_hbm.at[blocks], out_sems.at[i]))
        arrive[i].start()
    squares = jnp.zeros((8, LANES), jnp.float32)
    for i in range(steps):
        arrive[i].wait()
        for pair in range(i * owners // 2, (i + 1) * owners // 2):
            lanes = slice(LANES * pair, LANES * (pair + 1))
            first, second = grad_ref[:middle, lanes], grad_ref[middle:, lanes]
            squares += jnp.sum((first * first + second * second).reshape(-1, 8, LANES), axis=0)
            block_ref[2 * pair] = low_halves(first, second).astype(jnp.bfloat16)
            block_ref[2 * pair + 1] = high_halves(first, second).astype(jnp.bfloat16)
        leave[i].start()
    square_ref[...] = jnp.sum(squares, axis=0, keepdims=True)
    for copy in leave:
        copy.wait()


def pack(grad_columns):
    columns, rows = grad_columns.shape
    steps = 4
    block = (rows // HALF, columns // 2, LANES)
    far = pl.BlockSpec(memory_space=pltpu.HBM)
    return pl.pallas_call(
        pack_kernel,
        in_specs=[far],
        out_specs=[far, pl.BlockSpec(memory_space=pltpu.VMEM)],
        out_shape=[jax.ShapeDtypeStruct(block, jnp.bfloat16), jax.ShapeDtypeStruct((1, LANES), jnp.float32)],
        scratch_shapes=[
            pltpu.VMEM((columns, rows), jnp.float32),
            pltpu.VMEM(block, jnp.bfloat16),
            pltpu.SemaphoreType.DMA((steps,)),
            pltpu.SemaphoreType.DMA((steps,)),
        ],
        compiler_params=pltpu.CompilerParams(vmem_limit_bytes=VMEM_LIMIT),
    )(pltpu.with_memory_space_constraint(grad_columns, pltpu.HBM))


def turn_kernel(grad_ref, master_hbm, first_hbm, second_hbm, turned_ref, master_ref, first_ref, second_ref, flat_ref, sems):
    held = ((master_hbm, master_ref), (first_hbm, first_ref), (second_hbm, second_ref))
    copies = [pltpu.make_async_copy(source, target, sems.at[k]) for k, (source, target) in enumerate(held)]
    for copy in copies:
        copy.start()
    middle, sources = grad_ref.shape[1], grad_ref.shape[0] // CHUNKS
    squares = turned_ref.shape[0] // CHUNKS
    for i in range(CHUNKS):
        for s in range(sources // 2):
            low = grad_ref[sources * i + s].astype(jnp.float32)
            high = grad_ref[sources * i + sources // 2 + s].astype(jnp.float32)
            at = 2 * middle * s
            flat_ref[at : at + middle] = low_halves(low, high)
            flat_ref[at + middle : at + 2 * middle] = high_halves(low, high)
        for j in range(squares):
            turned_ref[squares * i + j] = flat_ref[LANES * j : LANES * (j + 1)].T
    for copy in copies:
        copy.wait()


def turn(grad_blocks, *states):
    near, far = pl.BlockSpec(memory_space=pltpu.VMEM), pl.BlockSpec(memory_space=pltpu.HBM)
    state = jax.ShapeDtypeStruct(states[0].shape, jnp.float32)
    return pl.pallas_call(
        turn_kernel,
        in_specs=[near, far, far, far],
        out_specs=[near] * 4,
        out_shape=[jax.ShapeDtypeStruct((D // LANES // 2, LANES, LANES), jnp.float32)] + [state] * 3,
        scratch_shapes=[pltpu.VMEM((D // CHUNKS // 2, LANES), jnp.float32), pltpu.SemaphoreType.DMA((3,))],
        compiler_params=pltpu.CompilerParams(vmem_limit_bytes=VMEM_LIMIT),
    )(grad_blocks, *[pltpu.with_memory_space_constraint(a, pltpu.HBM) for a in states])


def adam_weights(gradient, master, first_moment, second_moment, factor):
    scaled = factor * gradient
    first_new = first_decay * first_moment + (1.0 - first_decay) * scaled
    second_new = second_decay * second_moment + (1.0 - second_decay) * scaled * scaled
    update = first_new / first_bias / (jnp.sqrt(second_new / second_bias) + epsilon)
    return shrink * master - learn_rate * update


def adam_kernel(entries, squares_ref, turned_ref, master_ref, first_ref, second_ref, out_ref, flat_ref):
    square_total = jnp.sum(squares_ref[...])
    factor = jnp.minimum(1.0, clip_level / jnp.sqrt(square_total / entries + stabilizer))
    sources, middle = out_ref.shape[0] // CHUNKS, out_ref.shape[1]
    width, squares = D // CHUNKS, turned_ref.shape[0] // CHUNKS
    for i in range(CHUNKS):
        for j in range(squares):
            at = width * i + LANES * j
            beyond = at + width // 2
            both = lambda ref: jnp.concatenate([ref[:, at : at + LANES], ref[:, beyond : beyond + LANES]], axis=0)
            gradient = turned_ref[squares * i + j]
            weights = adam_weights(gradient, both(master_ref), both(first_ref), both(second_ref), factor)
            flat_ref[LANES * j : LANES * (j + 1)] = weights.T
        for s in range(sources // 2):
            at = 2 * middle * s
            first, second = flat_ref[at : at + middle], flat_ref[at + middle : at + 2 * middle]
            out_ref[sources * i + s] = low_halves(first, second).astype(jnp.bfloat16)
            out_ref[sources * i + sources // 2 + s] = high_halves(first, second).astype(jnp.bfloat16)


def adam(entries, squares, turned, *states):
    near = pl.BlockSpec(memory_space=pltpu.VMEM)
    rows, columns = states[0].shape
    return pl.pallas_call(
        functools.partial(adam_kernel, entries),
        in_specs=[near] * 5,
        out_specs=near,
        out_shape=jax.ShapeDtypeStruct((FF // rows, columns * rows // FF // 2, LANES), jnp.bfloat16),
        scratch_shapes=[pltpu.VMEM((D // CHUNKS // 2, LANES), jnp.float32)],
        compiler_params=pltpu.CompilerParams(vmem_limit_bytes=VMEM_LIMIT),
    )(squares, turned, *states)


def unpack_kernel(block_ref, low_ref, high_ref):
    for pair in range(block_ref.shape[0] // 2):
        lanes = slice(LANES * pair, LANES * (pair + 1))
        first = block_ref[2 * pair].astype(jnp.float32)
        second = block_ref[2 * pair + 1].astype(jnp.float32)
        low_ref[:, lanes] = low_halves(first, second).astype(jnp.bfloat16)
        high_ref[:, lanes] = high_halves(first, second).astype(jnp.bfloat16)


def unpack(blocks):
    peers, middle, _ = blocks.shape
    steps = 4
    half = pl.BlockSpec((middle, peers * HALF // steps), lambda i: (0, i))
    return pl.pallas_call(
        unpack_kernel,
        grid=(steps,),
        in_specs=[pl.BlockSpec((peers // steps, middle, LANES), lambda i: (i, 0, 0))],
        out_specs=[half, half],
        out_shape=[jax.ShapeDtypeStruct((middle, peers * HALF), jnp.bfloat16)] * 2,
        compiler_params=pltpu.CompilerParams(vmem_limit_bytes=VMEM_LIMIT),
    )(blocks)


def shift(array, chips):
    size = lax.axis_size("grp")
    return lax.ppermute(array, "grp", [(i, (i + 2 * chips) % size) for i in range(size)])


def other_core(array):
    return lax.ppermute(array, "grp", [(i, i ^ 1) for i in range(lax.axis_size("grp"))])


def place_kernel(keys, halves, slot_ref, *refs):
    held, out_ref, blank_ref, sems = refs[: len(keys) * halves], refs[-3], refs[-2], refs[-1]
    slots, columns = out_ref.shape[0], out_ref.shape[1] // halves
    me, chips = lax.axis_index("grp"), lax.axis_size("grp") // 2

    def copy(source, slot, half):
        target = out_ref.at[slot, pl.ds(half * columns, columns)]
        return pltpu.make_async_copy(source, target, sems.at[slot, half])

    if -1 in keys:
        blank_ref[...] = jnp.zeros_like(blank_ref)
    places = []
    for slot in range(slots):
        expert = slot_ref[slot]
        apart = (expert // 2 - me // 2 + chips) % chips
        places.append(jnp.where(expert < 0, -1, 2 * apart + (expert + me) % 2))
    for act in ("start", "wait"):
        for slot in range(slots):
            for at, key in enumerate(keys):

                @pl.when(places[slot] == key)
                def _():
                    for half in range(halves):
                        source = blank_ref if key < 0 else held[half * len(keys) + at]
                        getattr(copy(source, slot, half), act)()


def place(slot_ids, keys, experts, rollout=None):
    slots, halves = slot_ids.shape[0], len(experts)
    columns, rows = experts[0][keys[-1]].shape
    held = [half[key] if key >= 0 else half[keys[-1]] for half in experts for key in keys]
    extra = [] if rollout is None else [rollout]
    far = pl.BlockSpec(memory_space=pl.ANY)
    size = len(keys) * halves * columns * rows
    return pl.pallas_call(
        functools.partial(place_kernel, keys, halves),
        in_specs=[pl.BlockSpec(memory_space=pltpu.SMEM)] + [far] * (len(held) + len(extra)),
        out_specs=far,
        out_shape=jax.ShapeDtypeStruct((slots, halves * columns, rows), jnp.bfloat16),
        scratch_shapes=[pltpu.VMEM((columns, rows), jnp.bfloat16), pltpu.SemaphoreType.DMA((slots, halves))],
        input_output_aliases={1 + len(held): 0} if extra else {},
        cost_estimate=pl.CostEstimate(flops=0, bytes_accessed=COST * size, transcendentals=0),
        compiler_params=pltpu.CompilerParams(vmem_limit_bytes=VMEM_LIMIT),
    )(slot_ids, *held, *extra)


def from_others(partial, axis, masks):
    size = lax.axis_size(axis)
    return [lax.ppermute(partial, axis, [(i, i ^ mask) for i in range(size)]) for mask in masks]


def body(gradient, master, first_moment, second_moment, slot_expert):
    entries = lax.axis_size("grp") * master.shape[0] * FF * D
    slot_ids = slot_expert.reshape(-1)
    grad_blocks, squares = pack(jnp.swapaxes(gradient[0], 0, 1))
    grad_here = lax.all_to_all(grad_blocks, "fsdp", 0, 0, tiled=True)
    for axis, masks in EXCHANGES[:-1]:
        squares = sum(from_others(squares, axis, masks), squares)
    turned, *states = turn(grad_here, master[0], first_moment[0], second_moment[0])
    others, turned = lax.optimization_barrier((from_others(squares, *EXCHANGES[-1]), turned))
    squares = sum(others, squares)
    weights = adam(entries, squares, turned, *states)
    columns = lax.all_to_all(weights, "fsdp", 0, 0, tiled=True)
    low, high = unpack(columns)
    halves = [{0: low}, {0: high}]
    for half, onward in zip(halves, (1, -1)):
        half[2], half[6] = shift(half[0], -1), shift(half[0], 1)
        half[4] = shift(half[6] if onward > 0 else half[2], onward)
        half[1], half[3], half[7] = other_core(half[0]), other_core(half[2]), other_core(half[6])
    rollout = place(slot_ids, FIRST, halves)
    for half in halves:
        half[5] = other_core(half[4])
    rollout = place(slot_ids, SECOND, halves, rollout)
    return jnp.swapaxes(rollout, 1, 2)


def solution(mesh):
    in_specs = (
        P("grp", None, "fsdp"),
        P("grp", "fsdp", None),
        P("grp", "fsdp", None),
        P("grp", "fsdp", None),
        P("grp", None),
    )
    out_specs = P("grp", None, "fsdp")
    return jax.shard_map(body, mesh=mesh, in_specs=in_specs, out_specs=out_specs, check_vma=False)
```
